32 devices in a mesh: dp: 8 (over z, y), node: 4 (over x, core).
Axes of the slice: x: 2, y: 2, z: 4, core: 2. Of those that a mesh axis runs over, the one named last changes fastest.
Arguments:
- tokens_in: bfloat16 [8192, 4096], P('dp', 'node'), may hold values from -6 to 6
- out_grads: bfloat16 [8192, 4096], P('dp'), may hold values from -0.01171875 to 0.01171875
- left_old: float32 [4096, 4096], P('node', 'dp'), may hold values from -0.1 to 4.1, as said below
- right_old: float32 [4096, 4096], P('node', 'dp'), may hold values from -0.1 to 4.1, as said below
Outputs:
- left_out: float32 [4096, 4096], P('node', 'dp')
- right_out: float32 [4096, 4096], P('node', 'dp')
The draws below stay inside these ranges and needn't reach their ends.
Inputs may be any that keep to these rules, and one draw needn't show every extreme that they name: `left_old`: symmetric. `right_old`: symmetric.
All inputs are finite; a program needn't handle non-finite values.
Results may differ from the reference program's by a relative error of at most 0.0021.
Values may be sent and summed in bfloat16 or wider, within the bound.
No kernel may reach another device: no remote copies, remote signals or barrier semaphores. Data moves between devices by JAX's collectives and lax.ppermute only.
A program may use at most 128 MiB of HBM per device.

```python
import jax
import jax.numpy as jnp

BLOCK = 4096
TOKENS = 8192


def symmetric_statistic(key, spread):
    noise_key, diagonal_key = jax.random.split(key)
    noise_field = jax.random.uniform(noise_key, (BLOCK, BLOCK), jnp.float32, -0.1, 0.1)
    symmetric = (noise_field + noise_field.T) * 0.5
    diagonal = jnp.exp(jax.random.uniform(diagonal_key, (BLOCK,), jnp.float32, 0.0, spread))
    return symmetric + jnp.eye(BLOCK, dtype=jnp.float32) * diagonal[None, :]


def draw_left_old(key, part):
    key = jax.random.fold_in(key, 11)
    return symmetric_statistic(key, 1.386)


def draw_right_old(key, part):
    key = jax.random.fold_in(key, 23)
    return symmetric_statistic(key, 1.386)


def spiked(entries, rng, source, target, shards_of, factor):
    owner, partner = [(jnp.arange(entries.shape[axis_at]) // (entries.shape[axis_at] // shards_of)).reshape([-1 if axis == axis_at else 1 for axis in range(entries.ndim)]) for axis_at in (source, target)]
    chosen = jax.random.permutation(rng, shards_of)[partner]
    strong = (owner == chosen) | (owner == (partner + shards_of // 2) % shards_of)
    return jnp.where(strong, factor * entries, entries)


def block_levels(stream_key, dims, cuts, smallest, high):
    loudness, own = 1.0, jax.random.fold_in(stream_key, 6)
    for axis_at, shards_of in cuts:
        steps = jnp.exp(jax.random.uniform(jax.random.fold_in(own, axis_at), (shards_of,), jnp.float32, smallest / len(cuts), high / len(cuts)))
        loudness = loudness * jnp.repeat(steps, dims[axis_at] // shards_of).reshape([-1 if axis == axis_at else 1 for axis in range(len(dims))])
    return loudness


def centred(own_key, extent, deviation, bound, cuts=(), kind=jnp.bfloat16):
    gain = block_levels(own_key, extent, cuts, -0.22, 0.18) if cuts else 1.0
    entries = jax.random.normal(own_key, extent, jnp.float32) * deviation * gain
    return jnp.minimum(jnp.maximum(entries, -bound), bound).astype(kind)


def noise_with(rng, extent, scale, most, cuts, heavy, held_as=jnp.bfloat16):
    array = scale * jax.random.normal(rng, extent, jnp.float32)
    if cuts:
        array = array * block_levels(rng, extent, cuts, -0.22, 0.18)
    return jnp.clip(spiked(array, jax.random.fold_in(rng, 3), *heavy), -most, most).astype(held_as)


def setup_inputs(seed: int = 0) -> dict:
    splits = jax.random.split(jax.random.key(seed), 5)
    return {
        "tokens_in": centred(splits[0], (TOKENS, BLOCK), 1.0, 6.0, ((0, 8), (1, 4))),
        "out_grads": noise_with(splits[1], (TOKENS, BLOCK), (BLOCK * TOKENS // 64) ** -0.5, 0.01171875, ((0, 8),), (0, 1, 8, 2.0)),
        "left_old": draw_left_old(jax.random.fold_in(splits[4], 71), 0),
        "right_old": draw_right_old(jax.random.fold_in(splits[4], 71), 0),
    }


ema_decay = 0.95


def reference(tokens_in, out_grads, left_old, right_old):
    grad = jnp.dot(tokens_in.T, out_grads, preferred_element_type=jnp.float32)
    grad_half = grad.astype(jnp.bfloat16)
    left_new = jnp.dot(grad_half, grad_half.T, preferred_element_type=jnp.float32)
    right_new = jnp.dot(grad_half.T, grad_half, preferred_element_type=jnp.float32)
    left_out = ema_decay * left_old + (1.0 - ema_decay) * left_new
    right_out = ema_decay * right_old + (1.0 - ema_decay) * right_new
    return left_out, right_out
```

```python
import jax
import jax.numpy as jnp
from jax import lax
from jax.sharding import PartitionSpec as P

ema_decay = 0.95
halves = 2
wire_gain = 2.0**20


def contract_first(left, right):
    return lax.dot_general(
        left, right, (((0,), (0,)), ((), ())), preferred_element_type=jnp.float32
    )


def contract_last(left, right):
    return lax.dot_general(
        left, right, (((1,), (1,)), ((), ())), preferred_element_type=jnp.float32
    )


def to_wire(value):
    root = jnp.sqrt(jnp.abs(value) * wire_gain)
    return jnp.where(value < 0, -root, root).astype(jnp.float16)


def from_wire(sent):
    root = sent.astype(jnp.float32)
    return root * jnp.abs(root) * (1.0 / wire_gain)


def pick(blocks, index):
    return lax.dynamic_index_in_dim(blocks, index, 0, keepdims=False)


def after(values, *done):
    return lax.optimization_barrier((values, done))[0]


def shards(tokens_in, out_grads, left_old, right_old):
    nodes = lax.axis_size("node")
    ring = lax.axis_size("dp")
    pair = ring // nodes
    depth = ring // pair
    dp_index = lax.axis_index("dp")
    node = lax.axis_index("node")
    z, y = dp_index // pair, dp_index % pair
    tokens = tokens_in.shape[0]
    rows, width = left_old.shape
    part = width // halves
    half = pair * part

    def place(z, y):
        return jnp.where(y == 0, z, ring - 1 - z)

    def member(position):
        return jnp.where(
            position < depth, position * pair, (ring - 1 - position) * pair + 1
        )

    order = [k * pair for k in range(depth)] + [k * pair + 1 for k in reversed(range(depth))]
    position = place(z, y)
    steps = ring // 2

    def rise(block):
        return lax.ppermute(
            block, "dp", [(order[k], order[(k + 1) % ring]) for k in range(ring)]
        )

    def fall(block):
        return lax.ppermute(
            block, "dp", [(order[(k + 1) % ring], order[k]) for k in range(ring)]
        )

    def swap(block):
        return lax.ppermute(block, "dp", [(d, d ^ 1) for d in range(ring)])

    def exchange(block, bit):
        return lax.ppermute(block, "node", [(n, n ^ bit) for n in range(nodes)])

    def spread(have):
        bit = nodes // 4
        while bit:
            for j in sorted(have):
                have[j | bit] = exchange(have[j], bit)
            bit //= 2
        return [have[j] for j in range(nodes)]

    tokens_split = tokens_in.reshape(tokens, pair, halves, part)
    own_tokens = [tokens_split[:, :, h].reshape(tokens, half) for h in range(halves)]

    def term(h, ahead):
        slab = member((position + ahead) % ring)
        grads = lax.dynamic_slice_in_dim(out_grads, slab * width, width, 1)
        return contract_first(own_tokens[h], grads)

    up, down = [None] * halves, [None] * halves

    def send_up(h, step):
        total = term(h, step)
        if up[h] is not None:
            total = total + from_wire(up[h])
        up[h] = rise(to_wire(total))

    def send_down(h, step):
        total = term(h, ring - step)
        if down[h] is not None:
            total = total + from_wire(down[h])
        down[h] = fall(to_wire(total))

    send_up(0, steps)
    send_down(1, steps)
    for step in range(steps - 1, 0, -1):
        send_up(1, step)
        send_down(0, step)
        send_up(0, step)
        send_down(1, step)
    own = [
        (term(h, 0) + from_wire(up[h]) + from_wire(down[h])).astype(jnp.bfloat16)
        for h in range(halves)
    ]

    sent = [{} for _ in range(halves)]

    def choose(h, panel, j, r):
        spot = (place(node ^ j, y ^ r) + ring - position) % ring
        sent[h][j, r] = pick(panel, spot)
        return sent[h][j, r]

    def gather(h, block, before, late):
        ups, downs, waiting = [block], [block], []

        def ahead():
            far = [ups[0]] if len(ups) <= steps else [jnp.concatenate([ups[-1], downs[-1]])]
            near = [block] + downs[1:steps] + far + ups[steps - 1 : 0 : -1]
            return jnp.stack(near)

        for step in range(1, steps + 1):
            top, bottom = ups[-1], downs[-1]
            if step == steps:
                top, bottom = top[: half // 2], bottom[half // 2 :]
            top, bottom = after((top, bottom), *waiting)
            waiting = []
            if step == steps:
                waiting = late(ahead(), (top, bottom))
            elif before:
                waiting = before.pop(0)((top, bottom))
            ups.append(rise(top))
            downs.append(fall(bottom))
        return ahead(), waiting

    top_bit = nodes // 2
    slab_far = [None] * halves

    def slab_job(h):
        def job(ready):
            slab_far[h] = exchange(after(own[h], ready), top_bit)
            return [slab_far[h]]

        return job

    cols = [{} for _ in range(halves)]

    def trade(h, panel, j, r):
        def job(ready):
            cols[h][j, r] = exchange(after(choose(h, panel, j, r), ready), j)
            return [cols[h][j, r]]

        return job

    far = [j for j in range(2, nodes)]
    first = far[0]

    def early(h):
        return lambda panel, ready: trade(h, panel, first, 0)(ready)

    panel_a, wait_a = gather(0, own[0], [slab_job(h) for h in range(halves)], early(0))
    slab = [spread({0: own[h], top_bit: slab_far[h]}) for h in range(halves)]

    jobs = [trade(0, panel_a, j, 0) for j in far[1:]] + [trade(0, panel_a, j, 1) for j in far]
    panel_b, wait_b = gather(1, after(own[1], panel_a, wait_a), jobs, early(1))
    ready = (panel_b, wait_b)
    for job in jobs:
        ready = job(ready)
    for j in far[1:]:
        ready = trade(1, panel_b, j, 0)(ready)
    for j in far:
        choose(1, panel_b, j, 1)
        cols[1][j, 1] = swap(cols[1][j, 0])
    for h, panel in ((0, panel_a), (1, panel_b)):
        for r in range(pair):
            cols[h][0, r] = choose(h, panel, 0, r)
            trade(h, panel, 1, r)(())

    mine = []
    for h in range(halves):
        piece = []
        for r in range(pair):
            found = jnp.stack([cols[h][j, r] for j in range(nodes)])
            found = lax.dynamic_slice(
                found, (z ^ node, y * part, 0), (1, part, width)
            )
            piece.append(found[0])
        piece = jnp.stack(piece)
        ready = exchange(after(piece, ready), top_bit)
        mine.append(spread({0: piece, top_bit: ready}))

    right_new = []
    for r in range(pair):
        total = 0.0
        for h in range(halves):
            for j in range(nodes):
                total = total + contract_first(cols[h][j, r], slab[h][j])
        right_new.append(total)
    right_new = jnp.concatenate(
        [
            jnp.where(y == 0, right_new[0], right_new[1]),
            jnp.where(y == 0, right_new[1], right_new[0]),
        ]
    )

    left_new = []
    for h in range(halves):
        line = []
        for g in range(halves):
            total = 0.0
            for j in range(nodes):
                for r in range(pair):
                    total = total + contract_last(sent[h][j, r], mine[g][j][r])
            line.append(total)
        left_new.append(jnp.concatenate(line, 1).reshape(pair, part, width))
    left_new = jnp.stack(left_new, 1).reshape(rows, width)
    left_out = ema_decay * left_old + (1.0 - ema_decay) * left_new
    right_out = ema_decay * right_old + (1.0 - ema_decay) * right_new
    return (left_out, right_out)


def solution(mesh):
    placed = (P("dp", "node"), P("dp", None), P("node", "dp"), P("node", "dp"))
    return jax.shard_map(
        shards,
        mesh=mesh,
        in_specs=placed,
        out_specs=(P("node", "dp"), P("node", "dp")),
        check_vma=False,
    )
```

```python
import functools

import jax
import jax.numpy as jnp
from jax import lax
from jax.experimental import pallas as pl
from jax.experimental.pallas import tpu as pltpu
from jax.sharding import PartitionSpec as P

ema_decay = 0.95
halves = 2
wire_gain = 2.0**20
kernel_vmem = 32 * 2**20
large_vmem = 56 * 2**20


def to_wire(value):
    scaled = value * wire_gain
    square = scaled * scaled
    return (scaled * jnp.abs(scaled) * square).astype(jnp.bfloat16)


def from_wire(sent):
    power = sent.astype(jnp.float32)
    root = lax.rsqrt(lax.rsqrt(jnp.abs(power))) * (1.0 / wire_gain)
    return jnp.where(power < 0, -root, root)


def after(values, *done):
    return lax.optimization_barrier((values, done))[0]


def sum_body(counts, parts, turned, slabs, tokens, first, second, *rest):
    arrived, outs = rest[: sum(counts)], rest[sum(counts) :]
    contracted = 1 if turned else 0
    for k, grads in enumerate((first, second)):
        total = lax.dot_general(
            tokens[...],
            grads[...],
            (((contracted,), (0,)), ((), ())),
            preferred_element_type=jnp.float32,
        )
        across = outs[k].shape[1]
        if total.shape[1] != across:
            total = total[:, parts[k] * across : (parts[k] + 1) * across]
        for ref in arrived[sum(counts[:k]) : sum(counts[: k + 1])]:
            total = total + from_wire(ref[...])
        outs[k][...] = to_wire(total) if outs[k].dtype == jnp.bfloat16 else total


def sum_round(slabs, tokens, turned, grads, half, picks, arrived, kind=jnp.bfloat16):
    rows, depth = tokens.shape if turned else tokens.shape[::-1]
    high = rows // 2 if rows % 512 == 0 else rows
    wide = half if half % 128 == 0 else half * halves
    per_slab = half * halves // wide
    parts = [part for _, part in picks]

    def grad_block(ahead, part):
        return pl.BlockSpec(
            (depth, wide), lambda i, s: (0, s[ahead] * per_slab + part % per_slab)
        )

    if turned:
        token_block = pl.BlockSpec((high, depth), lambda i, s: (i, 0))
    else:
        token_block = pl.BlockSpec((depth, high), lambda i, s: (0, i))
    block = pl.BlockSpec((high, half), lambda i, s: (i, 0))
    counts = tuple(len(a) for a in arrived)
    flat = [a for group in arrived for a in group]
    return pl.pallas_call(
        functools.partial(sum_body, counts, parts, turned),
        out_shape=[jax.ShapeDtypeStruct((rows, half), kind)] * 2,
        grid_spec=pltpu.PrefetchScalarGridSpec(
            num_scalar_prefetch=1,
            grid=(rows // high,),
            in_specs=[token_block] + [grad_block(*pick) for pick in picks] + [block] * len(flat),
            out_specs=[block] * 2,
        ),
        compiler_params=pltpu.CompilerParams(vmem_limit_bytes=kernel_vmem if turned else large_vmem),
        cost_estimate=pl.CostEstimate(
            flops=4 * half * depth * rows,
            bytes_accessed=2 * depth * rows + 4 * depth * half + 4 * half * rows * 2,
            transcendentals=0,
        ),
    )(slabs, tokens, grads, grads, *flat)


def block_spec(block, shape, where):
    array, index = block
    if index is None:
        return pl.BlockSpec(shape, where)
    return pl.BlockSpec((None, *shape), lambda *args: (index, *where(*args)))


def alone(block):
    array, index = block
    return array if index is None else array[index]


def pick_body(cases, count, spots, *refs):
    sources, out, sems = refs[:cases], refs[cases], refs[-1]
    for k in range(count):
        for c in range(cases):

            @pl.when(spots[k] == c)
            def _():
                pltpu.make_async_copy(sources[c], out.at[k], sems.at[k]).start()

    for k in range(count):
        pltpu.make_async_copy(sources[0], out.at[k], sems.at[k]).wait()


def pick_blocks(spots, cases):
    count = spots.shape[0]
    shape = (count, *cases[0].shape)
    return pl.pallas_call(
        functools.partial(pick_body, len(cases), count),
        out_shape=jax.ShapeDtypeStruct(shape, cases[0].dtype),
        grid_spec=pltpu.PrefetchScalarGridSpec(
            num_scalar_prefetch=1,
            grid=(1,),
            in_specs=[pl.BlockSpec(memory_space=pl.ANY)] * len(cases),
            out_specs=pl.BlockSpec(shape, lambda i, s: (0, 0, 0)),
            scratch_shapes=[pltpu.SemaphoreType.DMA((count,))],
        ),
        compiler_params=pltpu.CompilerParams(vmem_limit_bytes=kernel_vmem),
        cost_estimate=pl.CostEstimate(
            flops=0, bytes_accessed=4 * count * cases[0].size, transcendentals=0
        ),
    )(spots, *cases)


def rows_body(views, pair, high, spots, *refs):
    sources, out, sems = refs[: len(views)], refs[-2], refs[-1]
    start = pl.multiple_of(spots[1] * high, high)

    def rows(k, first):
        if views[k] is None:
            return sources[k].at[pl.ds(first, high)]
        return sources[k].at[views[k], pl.ds(first, high)]

    for r in range(pair):
        for c in range(len(views) // pair):

            @pl.when(spots[0] == c)
            def _():
                copied = rows(c * pair + r, start)
                pltpu.make_async_copy(copied, out.at[r], sems.at[r]).start()

    for r in range(pair):
        pltpu.make_async_copy(rows(r, 0), out.at[r], sems.at[r]).wait()


def pick_rows(spots, cases, pair, high):
    across, kind = cases[0][0].shape[-1], cases[0][0].dtype
    shape = (pair, high, across)
    return pl.pallas_call(
        functools.partial(rows_body, [view for _, view in cases], pair, high),
        out_shape=jax.ShapeDtypeStruct(shape, kind),
        grid_spec=pltpu.PrefetchScalarGridSpec(
            num_scalar_prefetch=1,
            grid=(1,),
            in_specs=[pl.BlockSpec(memory_space=pl.ANY)] * len(cases),
            out_specs=pl.BlockSpec(shape, lambda i, s: (0, 0, 0)),
            scratch_shapes=[pltpu.SemaphoreType.DMA((pair,))],
        ),
        compiler_params=pltpu.CompilerParams(vmem_limit_bytes=kernel_vmem),
        cost_estimate=pl.CostEstimate(
            flops=0, bytes_accessed=4 * pair * high * across, transcendentals=0
        ),
    )(spots, *[array for array, _ in cases])


def left_body(count, pair, final, *refs):
    blocks, theirs = refs[: count * pair], refs[count * pair : count * pair + count]
    rest = refs[count * pair + count :]
    total = rest[0][...] if len(rest) > 1 else 0.0
    for j in range(count):
        for r in range(pair):
            total = total + lax.dot_general(
                blocks[j * pair + r][...],
                theirs[j][r],
                (((1,), (1,)), ((), ())),
                preferred_element_type=jnp.float32,
            )
    if final:
        total = ema_decay * rest[1][...] + (1.0 - ema_decay) * total
    rest[-1][...] = total


def left_sum(blocks, theirs, earlier, final=False):
    rows, across = blocks[0][0].shape[-2:]
    width = theirs[0].shape[1]
    high = rows // 2 if rows % 512 == 0 else rows
    pair = len(blocks) // len(theirs)
    out = pl.BlockSpec((high, width), lambda i: (i, 0))
    return pl.pallas_call(
        functools.partial(left_body, len(theirs), pair, final),
        out_shape=jax.ShapeDtypeStruct((rows, width), jnp.float32),
        grid=(rows // high,),
        in_specs=[block_spec(b, (high, across), lambda i: (i, 0)) for b in blocks]
        + [pl.BlockSpec(theirs[0].shape, lambda i: (0, 0, 0))] * len(theirs)
        + [out] * len(earlier),
        out_specs=out,
        compiler_params=pltpu.CompilerParams(vmem_limit_bytes=large_vmem),
        cost_estimate=pl.CostEstimate(
            flops=2 * len(blocks) * across * rows * width,
            bytes_accessed=2 * len(blocks) * across * (rows + width) + 8 * rows * width,
            transcendentals=0,
        ),
    )(*[b for b, _ in blocks], *theirs, *earlier)


def turn_body(count, *refs):
    for k in range(count):
        refs[count + k][...] = refs[k][...].T


def turn_blocks(blocks):
    rows, across = blocks[0].shape
    high = min(rows, 256)
    return pl.pallas_call(
        functools.partial(turn_body, len(blocks)),
        out_shape=[jax.ShapeDtypeStruct((across, rows), blocks[0].dtype)] * len(blocks),
        grid=(rows // high,),
        in_specs=[pl.BlockSpec((high, across), lambda i: (i, 0))] * len(blocks),
        out_specs=[pl.BlockSpec((across, high), lambda i: (0, i))] * len(blocks),
        compiler_params=pltpu.CompilerParams(vmem_limit_bytes=large_vmem),
        cost_estimate=pl.CostEstimate(
            flops=0, bytes_accessed=4 * len(blocks) * rows * across, transcendentals=0
        ),
    )(*blocks)


def right_body(count, pair, *refs):
    slabs, blocks = refs[: count * halves], refs[count * halves : -2]
    out, total = refs[-2:]
    step = pl.program_id(0)

    @pl.when(step == 0)
    def _():
        total[...] = jnp.zeros_like(total)

    high = slabs[0].shape[0]
    for r in range(pair):
        for g in range(halves):
            part = 0.0
            for j in range(count):
                part = part + jnp.dot(
                    slabs[j * halves + g][...],
                    blocks[j * pair + r][...],
                    preferred_element_type=jnp.float32,
                )
            total[r, g * high : (g + 1) * high] += part

    @pl.when(step == pl.num_programs(0) - 1)
    def _():
        for r in range(pair):
            out[r] = total[r].T


def right_sum(slabs, blocks, pair):
    half, rows = slabs[0].shape
    count = len(blocks) // pair
    deep = rows // 2 if rows % 512 == 0 else rows
    return pl.pallas_call(
        functools.partial(right_body, count, pair),
        out_shape=jax.ShapeDtypeStruct((pair, half, half * halves), jnp.float32),
        grid=(rows // deep,),
        in_specs=[pl.BlockSpec((half, deep), lambda i: (0, i))] * len(slabs)
        + [block_spec(b, (deep, half), lambda i: (i, 0)) for b in blocks],
        out_specs=pl.BlockSpec((pair, half, half * halves), lambda i: (0, 0, 0)),
        scratch_shapes=[pltpu.VMEM((pair, half * halves, half), jnp.float32)],
        compiler_params=pltpu.CompilerParams(vmem_limit_bytes=large_vmem),
        cost_estimate=pl.CostEstimate(
            flops=2 * len(blocks) * half * rows * half * halves,
            bytes_accessed=2 * (len(blocks) + len(slabs)) * half * rows,
            transcendentals=0,
        ),
    )(*slabs, *[b for b, _ in blocks])


def shards(tokens_in, out_grads, left_old, right_old):
    nodes = lax.axis_size("node")
    ring = lax.axis_size("dp")
    pair = ring // nodes
    depth = ring // pair
    dp_index = lax.axis_index("dp")
    node = lax.axis_index("node")
    z, y = dp_index // pair, dp_index % pair
    width = left_old.shape[1]
    half = width // halves
    steps = ring // 2
    top_bit = nodes // 2

    def place(z, y):
        return jnp.where(y == 0, z, ring - 1 - z)

    order = [k * pair for k in range(depth)] + [k * pair + 1 for k in reversed(range(depth))]
    position = place(z, y)
    places = (position + jnp.arange(ring, dtype=jnp.int32)) % ring
    slabs = jnp.where(places < depth, places * pair, (ring - 1 - places) * pair + 1)

    def rise(block):
        return lax.ppermute(
            block, "dp", [(order[k], order[(k + 1) % ring]) for k in range(ring)]
        )

    def fall(block):
        return lax.ppermute(
            block, "dp", [(order[(k + 1) % ring], order[k]) for k in range(ring)]
        )

    def swap(block):
        return lax.ppermute(block, "dp", [(d, d ^ 1) for d in range(ring)])

    def exchange(bit):
        pairs = [(n, n ^ bit) for n in range(nodes)]
        return lambda block: lax.ppermute(block, "node", pairs)

    turned = tokens_in.T
    up, down = [None] * halves, [None] * halves
    previous = ()

    def send(h, up_step, down_step):
        nonlocal previous
        arrived = [[a[g]] if a[g] is not None else [] for a, g in ((up, h), (down, 1 - h))]
        picks = [(up_step, h), (ring - down_step, 1 - h)]
        turn = after(slabs, previous)
        tokens, flipped = (turned, True) if any(arrived) else (tokens_in, False)
        previous = sum_round(turn, tokens, flipped, out_grads, half, picks, arrived)
        up[h], down[1 - h] = rise(previous[0]), fall(previous[1])

    send(0, steps, steps)
    for step in range(steps - 1, 0, -1):
        send(1, step, step)
        send(0, step, step)
    turn = after(slabs, previous)
    last = sum_round(
        turn, turned, True, out_grads, half, [(0, 0), (0, 1)], [[], []], jnp.float32
    )
    own = [
        (last[h] + from_wire(up[h]) + from_wire(down[h])).astype(jnp.bfloat16)
        for h in range(halves)
    ]

    ups, downs = [[block] for block in own], [[block] for block in own]
    sent = [{} for _ in range(halves)]
    cols = [{} for _ in range(halves)]
    slab = [{0: (block, None)} for block in own]
    mine = [{} for _ in range(halves)]
    ended = ()
    near = []

    def choose(h, r, js, *done):
        bands = node ^ jnp.array(js, jnp.int32)
        spots = (place(bands, y ^ r) + ring - position) % ring
        middle = (ups, downs)[h][h][steps] if r else own[h]
        cases = downs[h][:steps] + [middle] + ups[h][steps - 1 : 0 : -1]
        picked = pick_blocks(after(spots, *done), cases)
        for k, j in enumerate(js):
            sent[h][j, r] = (picked, k)
            if j == 0:
                cols[h][0, r] = (picked, k)
            if j == 1:
                near.append((sent[h], (1, r), cols[h], (1, r), 1))
        return picked

    def slot(*jobs):
        nonlocal ended
        jobs = list(jobs)
        ready = [k for k, job in enumerate(near) if job[1] in job[0]][:3]
        taken = [near[k] for k in ready]
        near[:] = [job for k, job in enumerate(near) if k not in ready]
        for source, key, store, place_in, bit in taken:
            jobs.append((exchange(bit), alone(source[key]), keep(store, place_in)))
        ended = tuple(job[0](after(job[1], ended)) for job in jobs)
        for job, result in zip(jobs, ended):
            job[2](result)

    def keep(store, key):
        return lambda result: store.__setitem__(key, (result, None))

    def spread(store):
        have, bit = [0, top_bit], nodes // 4
        while bit:
            for j in sorted(have):
                near.append((store, j, store, j | bit, bit))
                have.append(j | bit)
            bit //= 2

    passing = [{} for _ in range(halves)]

    def pass_on(h, j, r):
        near.append((passing[h], (j, r), cols[h], (j, r), 1))

    def trade(h, r, js):
        def store(result):
            for k, j in enumerate(js):
                (passing if j & 1 else cols)[h][j, r] = (result, k)
                if j & 1:
                    pass_on(h, j, r)

        return (exchange(js[0] & ~1), choose(h, r, js), store)

    everyone = range(nodes)
    far = list(range(2, nodes))
    queue = [(r, [j, j + 1]) for r in range(pair) for j in far[::2]]
    jobs = {h + 1: (exchange(top_bit), own[h], keep(slab[h], top_bit)) for h in range(halves)}
    for h in range(halves):
        spread(slab[h])
    rounds = ring - 1
    holding = None
    for k in range(1, rounds + 1):
        h_up, h_down = int(k > steps), int(k >= steps)
        beside = [jobs[k]] if k in jobs else []
        ring_jobs = [
            (rise, ups[h_up][-1], ups[h_up].append),
            (fall, downs[h_down][-1], downs[h_down].append),
        ]
        if k >= steps and (k - steps) % 2 == 0 and queue:
            job = trade(0, *queue.pop(0))
            holding = (job[0](after(job[1], ended)), job[2])
        slot(*ring_jobs, *beside)
        if holding and (k - steps) % 2:
            holding[1](holding[0])
            ended = ended + (holding[0],)
            holding = None
        if k == steps + 1:
            for r in range(pair):
                choose(0, r, [0, 1], ended)
    if holding:
        holding[1](holding[0])
        ended = ended + (holding[0],)
    while queue:
        slot(trade(0, *queue.pop(0)))
    swaps = []

    def swap_job(j):
        store = passing if j & 1 else cols
        if j & 1:
            pass_on(1, j, 1)
        return (swap, alone(store[1][j, 0]), keep(store[1], (j, 1)))

    turned_slab = None
    for j in reversed(far):
        slot(trade(1, 0, [j]), *swaps)
        if turned_slab is None:
            choose(1, 0, [0, 1], ended[:0], sent[1][j, 0][0])
            choose(1, 1, [0, 1], sent[1][1, 0][0])
            whole_slab = [alone(slab[g][j]) for j in everyone for g in range(halves)]
            turned_slab = turn_blocks(after(whole_slab, sent[1][1, 1][0]))
        swaps = [swap_job(j)]
    choose(1, 1, far, ended)

    def own_rows(h):
        cases = [cols[h][j, r] for j in range(nodes) for r in range(pair)]
        piece = pick_rows(jnp.stack([z ^ node, y]), cases, pair, width)
        mine[h][0] = (piece, None)
        spread(mine[h])
        return (exchange(top_bit), piece, keep(mine[h], top_bit))

    def left_part(h, js, earlier, final=False):
        blocks = [sent[h][j, r] for j in js for r in range(pair)]
        return left_sum(blocks, [mine[h][j][0] for j in js], earlier, final)

    def complete(h):
        return all((j, r) in cols[h] for j in range(nodes) for r in range(pair))

    def right_part(h):
        return right_sum(
            turned_slab, [cols[h][j, r] for j in everyone for r in range(pair)], pair
        )

    while not complete(0):
        slot()
    right_new = [right_part(0)]
    job = own_rows(0)
    slot(job, *swaps)
    ended = ended + (right_new[0],)
    while not complete(1):
        slot()
    job = own_rows(1)
    slot(job)
    right_new.append(right_part(1))
    ended = ended + (right_new[1],)
    while not all(j in mine[0] for j in everyone):
        slot()
    total = left_part(0, everyone, [])
    ended = ended + (total,)
    while near:
        slot()
    total = left_part(1, everyone[:top_bit], [total])
    left_out = left_part(1, everyone[top_bit:], [total, left_old], True)

    right_new = jnp.stack(right_new, 1)
    right_new = jnp.where(y == 0, right_new, right_new[::-1]).reshape(right_old.shape)
    right_out = ema_decay * right_old + (1.0 - ema_decay) * right_new
    return (left_out, right_out)


def solution(mesh):
    placed = (P("dp", "node"), P("dp", None), P("node", "dp"), P("node", "dp"))
    return jax.shard_map(
        shards,
        mesh=mesh,
        in_specs=placed,
        out_specs=(P("node", "dp"), P("node", "dp")),
        check_vma=False,
    )
```

```python
import functools

import jax
import jax.numpy as jnp
from jax import lax
from jax.experimental import pallas as pl
from jax.experimental.pallas import tpu as pltpu
from jax.sharding import PartitionSpec as P

ema_decay = 0.95
halves = 2
wire_gain = 2.0**20
all_vmem = 60 * 2**20


def to_wire(value):
    scaled = value * wire_gain
    square = scaled * scaled
    return (scaled * jnp.abs(scaled) * square).astype(jnp.bfloat16)


def from_wire(sent):
    power = sent.astype(jnp.float32)
    root = lax.rsqrt(lax.rsqrt(jnp.abs(power))) * (1.0 / wire_gain)
    return jnp.where(power < 0, -root, root)


def pinned(arrays):
    return [pltpu.with_memory_space_constraint(a, pltpu.HBM) for a in arrays]


def after(values, *done):
    return lax.optimization_barrier((values, done))[0]


def sum_body(counts, parts, slabs, tokens, first, second, *rest):
    arrived, outs = rest[: sum(counts)], rest[sum(counts) :]
    for k, grads in enumerate((first, second)):
        total = lax.dot_general(
            tokens[...],
            grads[...],
            (((0,), (0,)), ((), ())),
            preferred_element_type=jnp.float32,
        )
        across = outs[k].shape[1]
        if total.shape[1] != across:
            total = total[:, parts[k] * across : (parts[k] + 1) * across]
        for ref in arrived[sum(counts[:k]) : sum(counts[: k + 1])]:
            total = total + from_wire(ref[...])
        outs[k][...] = to_wire(total) if outs[k].dtype == jnp.bfloat16 else total


def sum_round(slabs, tokens, grads, half, picks, arrived, kind=jnp.bfloat16):
    depth, rows = tokens.shape
    high = rows // 2 if rows % 512 == 0 else rows
    wide = half if half % 128 == 0 else half * halves
    per_slab = half * halves // wide
    parts = [part for _, part in picks]

    def grad_block(ahead, part):
        return pl.BlockSpec(
            (depth, wide), lambda i, s: (0, s[ahead] * per_slab + part % per_slab)
        )

    token_block = pl.BlockSpec((depth, high), lambda i, s: (0, i))
    block = pl.BlockSpec((high, half), lambda i, s: (i, 0))
    counts = tuple(len(a) for a in arrived)
    flat = [a for group in arrived for a in group]
    return pl.pallas_call(
        functools.partial(sum_body, counts, parts),
        out_shape=[jax.ShapeDtypeStruct((rows, half), kind)] * 2,
        grid_spec=pltpu.PrefetchScalarGridSpec(
            num_scalar_prefetch=1,
            grid=(rows // high,),
            in_specs=[token_block] + [grad_block(*pick) for pick in picks] + [block] * len(flat),
            out_specs=[block] * 2,
        ),
        compiler_params=pltpu.CompilerParams(vmem_limit_bytes=16 * 2**20),
        cost_estimate=pl.CostEstimate(
            flops=4 * half * depth * rows,
            bytes_accessed=0,
            transcendentals=0,
        ),
    )(slabs, tokens, *pinned([grads, grads]), *flat)


def block_spec(block, shape, where):
    array, index = block
    if index is None:
        return pl.BlockSpec(shape, where)
    return pl.BlockSpec((None, *shape), lambda *args: (index, *where(*args)))


def alone(block):
    array, index = block
    return array if index is None else array[index]


def pick_body(cases, groups, spots, *refs):
    sources, outs, sems = refs[:cases], list(refs[cases:-1]), refs[-1]
    targets = []
    for count, stacked in groups:
        if stacked:
            stack = outs.pop(0)
            targets += [stack.at[k] for k in range(count)]
        else:
            targets += [outs.pop(0) for _ in range(count)]
    for k, target in enumerate(targets):
        for c in range(cases):

            @pl.when(spots[k] == c)
            def _():
                pltpu.make_async_copy(sources[c], target, sems.at[k]).start()

    for k, target in enumerate(targets):
        pltpu.make_async_copy(sources[0], target, sems.at[k]).wait()


def pick_blocks(spots, cases, groups):
    total = spots.shape[0]
    shape = cases[0].shape
    shapes = []
    for count, stacked in groups:
        shapes += [(count, *shape)] if stacked else [shape] * count
    return pl.pallas_call(
        functools.partial(pick_body, len(cases), groups),
        out_shape=[jax.ShapeDtypeStruct(s, cases[0].dtype) for s in shapes],
        grid_spec=pltpu.PrefetchScalarGridSpec(
            num_scalar_prefetch=1,
            grid=(1,),
            in_specs=[pl.BlockSpec(memory_space=pl.ANY)] * len(cases),
            out_specs=[
                pl.BlockSpec(s, lambda i, p, s=s: (0,) * len(s)) for s in shapes
            ],
            scratch_shapes=[pltpu.SemaphoreType.DMA((total,))],
        ),
        compiler_params=pltpu.CompilerParams(vmem_limit_bytes=all_vmem),
    )(spots, *cases)


def rows_body(views, pair, high, spots, *refs):
    sources, out, sems = refs[: len(views)], refs[-2], refs[-1]
    start = pl.multiple_of(spots[1] * high, high)

    def rows(k, first):
        if views[k] is None:
            return sources[k].at[pl.ds(first, high)]
        return sources[k].at[views[k], pl.ds(first, high)]

    for r in range(pair):
        for c in range(len(views) // pair):

            @pl.when(spots[0] == c)
            def _():
                copied = rows(c * pair + r, start)
                pltpu.make_async_copy(copied, out.at[r], sems.at[r]).start()

    for r in range(pair):
        pltpu.make_async_copy(rows(r, 0), out.at[r], sems.at[r]).wait()


def pick_rows(spots, cases, pair, high):
    across, kind = cases[0][0].shape[-1], cases[0][0].dtype
    shape = (pair, high, across)
    return pl.pallas_call(
        functools.partial(rows_body, [view for _, view in cases], pair, high),
        out_shape=jax.ShapeDtypeStruct(shape, kind),
        grid_spec=pltpu.PrefetchScalarGridSpec(
            num_scalar_prefetch=1,
            grid=(1,),
            in_specs=[pl.BlockSpec(memory_space=pl.ANY)] * len(cases),
            out_specs=pl.BlockSpec(shape, lambda i, s: (0, 0, 0)),
            scratch_shapes=[pltpu.SemaphoreType.DMA((pair,))],
        ),
        compiler_params=pltpu.CompilerParams(vmem_limit_bytes=all_vmem),
    )(spots, *[array for array, _ in cases])


def left_body(count, pair, first, *refs):
    blocks, theirs = refs[: count * pair], refs[count * pair : count * pair + count]
    earlier, out = refs[count * pair + count :]
    total = 0.0
    for j in range(count):
        for r in range(pair):
            total = total + lax.dot_general(
                blocks[j * pair + r][...],
                theirs[j][r],
                (((1,), (1,)), ((), ())),
                preferred_element_type=jnp.float32,
            )
    kept = ema_decay * earlier[...] if first else earlier[...]
    out[...] = kept + (1.0 - ema_decay) * total


def left_sum(blocks, theirs, earlier, first):
    rows, across = blocks[0][0].shape[-2:]
    width = theirs[0].shape[1]
    high = rows // 2 if rows % 512 == 0 else rows
    pair = len(blocks) // len(theirs)
    out = pl.BlockSpec((high, width), lambda i: (i, 0))
    return pl.pallas_call(
        functools.partial(left_body, len(theirs), pair, first),
        out_shape=jax.ShapeDtypeStruct((rows, width), jnp.float32),
        grid=(rows // high,),
        in_specs=[block_spec(b, (high, across), lambda i: (i, 0)) for b in blocks]
        + [pl.BlockSpec(theirs[0].shape, lambda i: (0, 0, 0))] * len(theirs)
        + [out],
        out_specs=out,
        compiler_params=pltpu.CompilerParams(vmem_limit_bytes=all_vmem),
        cost_estimate=pl.CostEstimate(
            flops=2 * len(blocks) * across * rows * width,
            bytes_accessed=0,
            transcendentals=0,
        ),
    )(*[b for b, _ in blocks], *theirs, earlier)


def turn_body(count, *refs):
    for k in range(count):
        refs[count + k][...] = refs[k][...].T


def turn_blocks(blocks):
    rows, across = blocks[0].shape
    high = min(rows, 256)
    return pl.pallas_call(
        functools.partial(turn_body, len(blocks)),
        out_shape=[pltpu.HBM((across, rows), blocks[0].dtype)] * len(blocks),
        grid=(rows // high,),
        in_specs=[pl.BlockSpec((high, across), lambda i: (i, 0))] * len(blocks),
        out_specs=[pl.BlockSpec((across, high), lambda i: (0, i))] * len(blocks),
        compiler_params=pltpu.CompilerParams(vmem_limit_bytes=all_vmem),
    )(*blocks)


def right_body(count, pair, *refs):
    slabs, blocks = refs[: count * halves], refs[count * halves : -2]
    out, total = refs[-2:]
    step = pl.program_id(0)

    @pl.when(step == 0)
    def _():
        total[...] = jnp.zeros_like(total)

    high = slabs[0].shape[0]
    for r in range(pair):
        for g in range(halves):
            part = 0.0
            for j in range(count):
                part = part + jnp.dot(
                    slabs[j * halves + g][...],
                    blocks[j * pair + r][...],
                    preferred_element_type=jnp.float32,
                )
            total[r, g * high : (g + 1) * high] += part

    @pl.when(step == pl.num_programs(0) - 1)
    def _():
        for r in range(pair):
            out[r] = total[r].T


def right_sum(slabs, blocks, pair):
    half, rows = slabs[0].shape
    count = len(blocks) // pair
    deep = rows // 2 if rows % 512 == 0 else rows
    return pl.pallas_call(
        functools.partial(right_body, count, pair),
        out_shape=jax.ShapeDtypeStruct((pair, half, half * halves), jnp.float32),
        grid=(rows // deep,),
        in_specs=[pl.BlockSpec((half, deep), lambda i: (0, i))] * len(slabs)
        + [block_spec(b, (deep, half), lambda i: (i, 0)) for b in blocks],
        out_specs=pl.BlockSpec((pair, half, half * halves), lambda i: (0, 0, 0)),
        scratch_shapes=[pltpu.VMEM((pair, half * halves, half), jnp.float32)],
        compiler_params=pltpu.CompilerParams(vmem_limit_bytes=all_vmem),
        cost_estimate=pl.CostEstimate(
            flops=2 * len(blocks) * half * rows * half * halves,
            bytes_accessed=0,
            transcendentals=0,
        ),
    )(*pinned(slabs), *[b for b, _ in blocks])


def shards(tokens_in, out_grads, left_old, right_old):
    nodes = lax.axis_size("node")
    ring = lax.axis_size("dp")
    pair = ring // nodes
    depth = ring // pair
    dp_index = lax.axis_index("dp")
    node = lax.axis_index("node")
    z, y = dp_index // pair, dp_index % pair
    width = left_old.shape[1]
    half = width // halves
    steps = ring // 2
    top_bit = nodes // 2

    def place(z, y):
        return jnp.where(y == 0, z, ring - 1 - z)

    order = [k * pair for k in range(depth)] + [k * pair + 1 for k in reversed(range(depth))]
    position = place(z, y)
    places = (position + jnp.arange(ring, dtype=jnp.int32)) % ring
    slabs = jnp.where(places < depth, places * pair, (ring - 1 - places) * pair + 1)

    def rise(block):
        return lax.ppermute(
            block, "dp", [(order[k], order[(k + 1) % ring]) for k in range(ring)]
        )

    def fall(block):
        return lax.ppermute(
            block, "dp", [(order[(k + 1) % ring], order[k]) for k in range(ring)]
        )

    def swap(block):
        return lax.ppermute(block, "dp", [(d, d ^ 1) for d in range(ring)])

    def exchange(bit):
        pairs = [(n, n ^ bit) for n in range(nodes)]
        return lambda block: lax.ppermute(block, "node", pairs)

    up, down = [None] * halves, [None] * halves
    previous = ()

    def send(h, up_step, down_step):
        nonlocal previous
        arrived = [[a[g]] if a[g] is not None else [] for a, g in ((up, h), (down, 1 - h))]
        picks = [(up_step, h), (ring - down_step, 1 - h)]
        turn = after(slabs, previous)
        previous = sum_round(turn, tokens_in, out_grads, half, picks, arrived)
        up[h], down[1 - h] = rise(previous[0]), fall(previous[1])

    send(0, steps, steps)
    for step in range(steps - 1, 0, -1):
        send(1, step, step)
        send(0, step, step)
    turn = after(slabs, previous)
    last = sum_round(
        turn, tokens_in, out_grads, half, [(0, 0), (0, 1)], [[], []], jnp.float32
    )
    def finish(h, *done):
        first = after(last[h], *done)
        return (first + from_wire(up[h]) + from_wire(down[h])).astype(jnp.bfloat16)

    own = [finish(0)]
    slab = [{0: (own[0], None)}]
    slab[0][1] = (exchange(1)(own[0]), None)
    own.append(finish(1, slab[0][1][0]))
    slab.append({0: (own[1], None)})

    ups, downs = [[block] for block in own], [[block] for block in own]
    sent = [{} for _ in range(halves)]
    cols = [{} for _ in range(halves)]
    mine = [{} for _ in range(halves)]
    ended = ()
    near = []

    def choose(h, wanted, *done):
        spots, groups = [], []
        for r, js in wanted:
            bands = node ^ jnp.array(js, jnp.int32)
            spots.append((place(bands, y ^ r) + ring - position) % ring)
            groups.append((len(js), len(js) > 1 and js[0] > 1))
        middle = (ups, downs)[h][h][steps:] or [own[h]]
        cases = downs[h][:steps] + middle + ups[h][steps - 1 : 0 : -1]
        picked = pick_blocks(after(jnp.concatenate(spots), *done), cases, groups)
        first = picked[0]
        for (r, js), (_, stacked) in zip(wanted, groups):
            if stacked:
                stack, picked = picked[0], picked[1:]
            for k, j in enumerate(js):
                if stacked:
                    sent[h][j, r] = (stack, k)
                else:
                    sent[h][j, r], picked = (picked[0], None), picked[1:]
                if j == 0:
                    cols[h][0, r] = sent[h][0, r]
                if j == 1:
                    near.append((sent[h], (1, r), cols[h], (1, r), 1))
        return first

    def take_near(most):
        ready = [k for k, job in enumerate(near) if job[1] in job[0]][:most]
        taken = [near[k] for k in ready]
        near[:] = [job for k, job in enumerate(near) if k not in ready]
        jobs = []
        for source, key, store, place_in, bit in taken:
            array, view = source[key]
            jobs.append((exchange(bit), array, keep(store, place_in, view)))
        return jobs

    def slot(*jobs):
        nonlocal ended
        jobs = list(jobs) + take_near(3)
        ended = tuple(job[0](after(job[1], ended)) for job in jobs)
        for job, result in zip(jobs, ended):
            job[2](result)

    def keep(store, key, view=None):
        return lambda result: store.__setitem__(key, (result, view))

    def spread(store):
        have, bit = [0, top_bit], nodes // 4
        while bit:
            for j in sorted(have):
                if j | bit not in store:
                    near.append((store, j, store, j | bit, bit))
                have.append(j | bit)
            bit //= 2

    passing = [{} for _ in range(halves)]

    def pass_on(h, j, r):
        near.append((passing[h], (j, r), cols[h], (j, r), 1))

    def trade(h, r, js):
        def store(result):
            for k, j in enumerate(js):
                view = (result, k) if len(js) > 1 else (result, None)
                (passing if j & 1 else cols)[h][j, r] = view
                if j & 1:
                    pass_on(h, j, r)

        array = sent[h][js[0], r][0]
        return (exchange(js[0] & ~1), array, store)

    everyone = range(nodes)
    far = list(range(2, nodes))
    queue = [(r, [j, j + 1]) for r in range(pair) for j in far[::2]]
    for h in range(halves):
        spread(slab[h])
    rounds = ring - 1
    gate, loose, holding = (), (), None
    for k in range(1, rounds + 1):
        h_up, h_down = int(k > steps), int(k >= steps)
        top, bottom = ups[h_up][-1], downs[h_down][-1]
        if k <= halves:
            far_own = after(own[k - 1], [g for g in loose[-1:]])
            far_own = exchange(top_bit)(far_own)
            slab[k - 1][top_bit] = (far_own, None)
            loose = loose + (far_own,)
        if k == steps:
            first_wanted, rest = queue[:1], queue[1:]
            choose(0, first_wanted)
        if k >= steps and (k - steps) % 2 == 0 and queue:
            operator, operand, store = trade(0, *queue.pop(0))
            holding = (operator(after(operand, loose)), store)
            loose = ()
        if k == 3 or k > steps + 1:
            for operator, operand, store in take_near(4):
                result = operator(after(operand, gate, top, bottom))
                store(result)
                loose = loose + (result,)
        top, bottom = after((top, bottom), gate)
        if k > steps and (k - steps) % 2:
            gate = (holding[0],) if holding else ()
            if holding:
                holding[1](holding[0])
                holding = None
            if k == steps + 1:
                gate += (choose(0, rest + [(r, [0, 1]) for r in range(pair)]),)
        else:
            gate = ()
        ups[h_up].append(rise(top))
        downs[h_down].append(fall(bottom))
    ended = (ups[1][-1], downs[1][-1], gate, loose)
    if holding:
        holding[1](holding[0])
        ended = ended + (holding[0],)
    while queue:
        slot(trade(0, *queue.pop(0)))
    swaps = []

    def swap_job(j):
        store = passing if j & 1 else cols
        if j & 1:
            pass_on(1, j, 1)
        array, view = store[1][j, 0]
        return (swap, array, keep(store[1], (j, 1), view))

    first = choose(1, [(0, far[-1:])])
    turned_slab = None
    for j in reversed(far):
        slot(trade(1, 0, [j]), *swaps)
        if turned_slab is None:
            single = [(0, [i]) for i in far[:-1]]
            wanted = single + [(r, [0, 1]) for r in range(pair)] + [(1, far)]
            first = choose(1, wanted, first)
            whole_slab = [alone(slab[g][j]) for j in everyone for g in range(halves)]
            turned_slab = turn_blocks(after(whole_slab, first))
        swaps = [swap_job(j)]

    def own_rows(h):
        cases = [cols[h][j, r] for j in range(nodes) for r in range(pair)]
        piece = pick_rows(jnp.stack([z ^ node, y]), cases, pair, width)
        mine[h][0] = (piece, None)
        spread(mine[h])
        return (exchange(top_bit), piece, keep(mine[h], top_bit))

    def left_part(parts, earlier, first=False):
        blocks = [sent[h][j, r] for h, js in parts for j in js for r in range(pair)]
        theirs = [mine[h][j][0] for h, js in parts for j in js]
        return left_sum(blocks, theirs, earlier, first)

    def complete(h):
        return all((j, r) in cols[h] for j in range(nodes) for r in range(pair))

    def right_part(h):
        return right_sum(
            turned_slab, [cols[h][j, r] for j in everyone for r in range(pair)], pair
        )

    while not complete(0):
        slot()
    right_new = [right_part(0)]
    job = own_rows(0)
    slot(job, *swaps)
    ended = ended + (right_new[0],)
    while not complete(1):
        slot()
    job = own_rows(1)
    slot(job)
    right_new.append(right_part(1))
    ended = ended + (right_new[1],)
    while not all(j in mine[0] for j in everyone):
        slot()
    lows, highs = list(everyone)[:top_bit], list(everyone)[top_bit:]
    total = left_part([(0, lows)], left_old, True)
    while not all(j in mine[1] for j in lows):
        slot()
    total = left_part([(0, highs), (1, lows)], total)
    ended = ended + (total,)
    while near:
        slot()
    left_out = left_part([(1, highs)], total)

    right_new = jnp.stack(right_new, 1)
    right_new = jnp.where(y == 0, right_new, right_new[::-1]).reshape(right_old.shape)
    right_out = ema_decay * right_old + (1.0 - ema_decay) * right_new
    return (left_out, right_out)


def solution(mesh):
    placed = (P("dp", "node"), P("dp", None), P("node", "dp"), P("node", "dp"))
    return jax.shard_map(
        shards,
        mesh=mesh,
        in_specs=placed,
        out_specs=(P("node", "dp"), P("node", "dp")),
        check_vma=False,
    )
```

```python
import functools

import jax
import jax.numpy as jnp
from jax import lax
from jax.experimental import pallas as pl
from jax.experimental.pallas import tpu as pltpu
from jax.sharding import PartitionSpec as P

ema_decay = 0.95
halves = 2
wire_gain = 2.0**31
all_vmem = 60 * 2**20


def to_wire(value):
    scaled = value * wire_gain
    return (scaled * scaled * scaled).astype(jnp.bfloat16)


def from_wire(sent):
    cube = sent.astype(jnp.float32)
    size = jnp.maximum(jnp.abs(cube), 2.0**-126)
    root = jnp.exp2(jnp.log2(size) * (1.0 / 3.0)) * (1.0 / wire_gain)
    return jnp.where(cube < 0, -root, root)


def pinned(arrays):
    return [pltpu.with_memory_space_constraint(a, pltpu.HBM) for a in arrays]


def after(values, *done):
    return lax.optimization_barrier((values, done))[0]


def sum_body(counts, parts, slabs, tokens, first, second, *rest):
    arrived, outs = rest[: sum(counts)], rest[sum(counts) :]
    for k, grads in enumerate((first, second)):
        total = lax.dot_general(
            tokens[...],
            grads[...],
            (((0,), (0,)), ((), ())),
            preferred_element_type=jnp.float32,
        )
        across = outs[k].shape[1]
        if total.shape[1] != across:
            total = total[:, parts[k] * across : (parts[k] + 1) * across]
        for ref in arrived[sum(counts[:k]) : sum(counts[: k + 1])]:
            total = total + from_wire(ref[...])
        outs[k][...] = to_wire(total) if outs[k].dtype == jnp.bfloat16 else total


def sum_round(slabs, tokens, grads, half, picks, arrived, kind=jnp.bfloat16):
    depth, rows = tokens.shape
    high = rows // 2 if rows % 512 == 0 else rows
    wide = half if half % 128 == 0 else half * halves
    per_slab = half * halves // wide
    parts = [part for _, part in picks]

    def grad_block(ahead, part):
        return pl.BlockSpec(
            (depth, wide), lambda i, s: (0, s[ahead] * per_slab + part % per_slab)
        )

    token_block = pl.BlockSpec((depth, high), lambda i, s: (0, i))
    block = pl.BlockSpec((high, half), lambda i, s: (i, 0))
    counts = tuple(len(a) for a in arrived)
    flat = [a for group in arrived for a in group]
    return pl.pallas_call(
        functools.partial(sum_body, counts, parts),
        out_shape=[jax.ShapeDtypeStruct((rows, half), kind)] * 2,
        grid_spec=pltpu.PrefetchScalarGridSpec(
            num_scalar_prefetch=1,
            grid=(rows // high,),
            in_specs=[token_block] + [grad_block(*pick) for pick in picks] + [block] * len(flat),
            out_specs=[block] * 2,
        ),
        compiler_params=pltpu.CompilerParams(vmem_limit_bytes=16 * 2**20),
        cost_estimate=pl.CostEstimate(
            flops=4 * half * depth * rows,
            bytes_accessed=0,
            transcendentals=0,
        ),
    )(slabs, tokens, *pinned([grads, grads]), *flat)


def block_spec(block, shape, where):
    array, index = block
    if index is None:
        return pl.BlockSpec(shape, where)
    return pl.BlockSpec((None, *shape), lambda *args: (index, *where(*args)))


def alone(block):
    array, index = block
    return array if index is None else array[index]


def pick_body(cases, groups, spots, *refs):
    sources, outs, sems = refs[:cases], list(refs[cases:-1]), refs[-1]
    targets = []
    for count, stacked in groups:
        if stacked:
            stack = outs.pop(0)
            targets += [stack.at[k] for k in range(count)]
        else:
            targets += [outs.pop(0) for _ in range(count)]
    for k, target in enumerate(targets):
        for c in range(cases):

            @pl.when(spots[k] == c)
            def _():
                pltpu.make_async_copy(sources[c], target, sems.at[k]).start()

    for k, target in enumerate(targets):
        pltpu.make_async_copy(sources[0], target, sems.at[k]).wait()


def pick_blocks(spots, cases, groups):
    total = spots.shape[0]
    shape = cases[0].shape
    shapes = []
    for count, stacked in groups:
        shapes += [(count, *shape)] if stacked else [shape] * count
    return pl.pallas_call(
        functools.partial(pick_body, len(cases), groups),
        out_shape=[jax.ShapeDtypeStruct(s, cases[0].dtype) for s in shapes],
        grid_spec=pltpu.PrefetchScalarGridSpec(
            num_scalar_prefetch=1,
            grid=(1,),
            in_specs=[pl.BlockSpec(memory_space=pl.ANY)] * len(cases),
            out_specs=[
                pl.BlockSpec(s, lambda i, p, s=s: (0,) * len(s)) for s in shapes
            ],
            scratch_shapes=[pltpu.SemaphoreType.DMA((total,))],
        ),
        compiler_params=pltpu.CompilerParams(vmem_limit_bytes=all_vmem),
    )(spots, *cases)


def rows_body(views, pair, high, spots, *refs):
    sources, out, sems = refs[: len(views)], refs[-2], refs[-1]
    start = pl.multiple_of(spots[1] * high, high)

    def rows(k, first):
        if views[k] is None:
            return sources[k].at[pl.ds(first, high)]
        return sources[k].at[views[k], pl.ds(first, high)]

    for r in range(pair):
        for c in range(len(views) // pair):

            @pl.when(spots[0] == c)
            def _():
                copied = rows(c * pair + r, start)
                pltpu.make_async_copy(copied, out.at[r], sems.at[r]).start()

    for r in range(pair):
        pltpu.make_async_copy(rows(r, 0), out.at[r], sems.at[r]).wait()


def pick_rows(spots, cases, pair, high):
    across, kind = cases[0][0].shape[-1], cases[0][0].dtype
    shape = (pair, high, across)
    return pl.pallas_call(
        functools.partial(rows_body, [view for _, view in cases], pair, high),
        out_shape=jax.ShapeDtypeStruct(shape, kind),
        grid_spec=pltpu.PrefetchScalarGridSpec(
            num_scalar_prefetch=1,
            grid=(1,),
            in_specs=[pl.BlockSpec(memory_space=pl.ANY)] * len(cases),
            out_specs=pl.BlockSpec(shape, lambda i, s: (0, 0, 0)),
            scratch_shapes=[pltpu.SemaphoreType.DMA((pair,))],
        ),
        compiler_params=pltpu.CompilerParams(vmem_limit_bytes=all_vmem),
    )(spots, *[array for array, _ in cases])


def left_body(count, pair, first, *refs):
    blocks, theirs = refs[: count * pair], refs[count * pair : count * pair + count]
    earlier, out = refs[count * pair + count :]
    total = 0.0
    for j in range(count):
        for r in range(pair):
            total = total + lax.dot_general(
                blocks[j * pair + r][...],
                theirs[j][r],
                (((1,), (1,)), ((), ())),
                preferred_element_type=jnp.float32,
            )
    kept = ema_decay * earlier[...] if first else earlier[...]
    out[...] = kept + (1.0 - ema_decay) * total


def left_sum(blocks, theirs, earlier, first):
    rows, across = blocks[0][0].shape[-2:]
    width = theirs[0].shape[1]
    high = rows // 2 if rows % 512 == 0 else rows
    pair = len(blocks) // len(theirs)
    out = pl.BlockSpec((high, width), lambda i: (i, 0))
    return pl.pallas_call(
        functools.partial(left_body, len(theirs), pair, first),
        out_shape=jax.ShapeDtypeStruct((rows, width), jnp.float32),
        grid=(rows // high,),
        in_specs=[block_spec(b, (high, across), lambda i: (i, 0)) for b in blocks]
        + [pl.BlockSpec(theirs[0].shape, lambda i: (0, 0, 0))] * len(theirs)
        + [out],
        out_specs=out,
        compiler_params=pltpu.CompilerParams(vmem_limit_bytes=all_vmem),
        cost_estimate=pl.CostEstimate(
            flops=2 * len(blocks) * across * rows * width,
            bytes_accessed=0,
            transcendentals=0,
        ),
    )(*[b for b, _ in blocks], *theirs, earlier)


def turn_body(count, *refs):
    for k in range(count):
        refs[count + k][...] = refs[k][...].T


def turn_blocks(blocks):
    rows, across = blocks[0].shape
    high = min(rows, 256)
    return pl.pallas_call(
        functools.partial(turn_body, len(blocks)),
        out_shape=[pltpu.HBM((across, rows), blocks[0].dtype)] * len(blocks),
        grid=(rows // high,),
        in_specs=[pl.BlockSpec((high, across), lambda i: (i, 0))] * len(blocks),
        out_specs=[pl.BlockSpec((across, high), lambda i: (0, i))] * len(blocks),
        compiler_params=pltpu.CompilerParams(vmem_limit_bytes=all_vmem),
    )(*blocks)


def right_body(count, pair, *refs):
    slabs, blocks = refs[: count * halves], refs[count * halves : -2]
    out, total = refs[-2:]
    step = pl.program_id(0)

    @pl.when(step == 0)
    def _():
        total[...] = jnp.zeros_like(total)

    high = slabs[0].shape[0]
    for r in range(pair):
        for g in range(halves):
            part = 0.0
            for j in range(count):
                part = part + jnp.dot(
                    slabs[j * halves + g][...],
                    blocks[j * pair + r][...],
                    preferred_element_type=jnp.float32,
                )
            total[r, g * high : (g + 1) * high] += part

    @pl.when(step == pl.num_programs(0) - 1)
    def _():
        for r in range(pair):
            out[r] = total[r].T


def right_sum(slabs, blocks, pair):
    half, rows = slabs[0].shape
    count = len(blocks) // pair
    deep = rows // 2 if rows % 512 == 0 else rows
    return pl.pallas_call(
        functools.partial(right_body, count, pair),
        out_shape=jax.ShapeDtypeStruct((pair, half, half * halves), jnp.float32),
        grid=(rows // deep,),
        in_specs=[pl.BlockSpec((half, deep), lambda i: (0, i))] * len(slabs)
        + [block_spec(b, (deep, half), lambda i: (i, 0)) for b in blocks],
        out_specs=pl.BlockSpec((pair, half, half * halves), lambda i: (0, 0, 0)),
        scratch_shapes=[pltpu.VMEM((pair, half * halves, half), jnp.float32)],
        compiler_params=pltpu.CompilerParams(vmem_limit_bytes=all_vmem),
        cost_estimate=pl.CostEstimate(
            flops=2 * len(blocks) * half * rows * half * halves,
            bytes_accessed=0,
            transcendentals=0,
        ),
    )(*pinned(slabs), *[b for b, _ in blocks])


def shards(tokens_in, out_grads, left_old, right_old):
    nodes = lax.axis_size("node")
    ring = lax.axis_size("dp")
    pair = ring // nodes
    depth = ring // pair
    dp_index = lax.axis_index("dp")
    node = lax.axis_index("node")
    z, y = dp_index // pair, dp_index % pair
    width = left_old.shape[1]
    half = width // halves
    steps = ring // 2
    top_bit = nodes // 2

    def place(z, y):
        return jnp.where(y == 0, z, ring - 1 - z)

    order = [k * pair for k in range(depth)] + [k * pair + 1 for k in reversed(range(depth))]
    position = place(z, y)
    places = (position + jnp.arange(ring, dtype=jnp.int32)) % ring
    slabs = jnp.where(places < depth, places * pair, (ring - 1 - places) * pair + 1)

    def rise(block):
        return lax.ppermute(
            block, "dp", [(order[k], order[(k + 1) % ring]) for k in range(ring)]
        )

    def fall(block):
        return lax.ppermute(
            block, "dp", [(order[(k + 1) % ring], order[k]) for k in range(ring)]
        )

    def swap(block):
        return lax.ppermute(block, "dp", [(d, d ^ 1) for d in range(ring)])

    def exchange(bit):
        pairs = [(n, n ^ bit) for n in range(nodes)]
        return lambda block: lax.ppermute(block, "node", pairs)

    up, down = [None] * halves, [None] * halves
    previous = ()

    def send(h, up_step, down_step):
        nonlocal previous
        arrived = [[a[g]] if a[g] is not None else [] for a, g in ((up, h), (down, 1 - h))]
        picks = [(up_step, h), (ring - down_step, 1 - h)]
        turn = after(slabs, previous)
        previous = sum_round(turn, tokens_in, out_grads, half, picks, arrived)
        up[h], down[1 - h] = rise(previous[0]), fall(previous[1])

    send(0, steps, steps)
    for step in range(steps - 1, 0, -1):
        send(1, step, step)
        send(0, step, step)
    turn = after(slabs, previous)
    last = sum_round(
        turn, tokens_in, out_grads, half, [(0, 0), (0, 1)], [[], []], jnp.float32
    )
    def finish(h, *done):
        first = after(last[h], *done)
        return (first + from_wire(up[h]) + from_wire(down[h])).astype(jnp.bfloat16)

    own = [finish(0)]
    slab = [{0: (own[0], None)}]
    slab[0][1] = (exchange(1)(own[0]), None)
    own.append(finish(1, slab[0][1][0]))
    slab.append({0: (own[1], None)})

    ups, downs = [[block] for block in own], [[block] for block in own]
    sent = [{} for _ in range(halves)]
    cols = [{} for _ in range(halves)]
    mine = [{} for _ in range(halves)]
    ended = ()
    near = []

    def choose(h, wanted, *done):
        spots, groups = [], []
        for r, js in wanted:
            bands = node ^ jnp.array(js, jnp.int32)
            spots.append((place(bands, y ^ r) + ring - position) % ring)
            groups.append((len(js), len(js) > 1 and js[0] > 1))
        middle = (ups, downs)[h][h][steps:] or [own[h]]
        cases = downs[h][:steps] + middle + ups[h][steps - 1 : 0 : -1]
        picked = pick_blocks(after(jnp.concatenate(spots), *done), cases, groups)
        first = picked[0]
        for (r, js), (_, stacked) in zip(wanted, groups):
            if stacked:
                stack, picked = picked[0], picked[1:]
            for k, j in enumerate(js):
                if stacked:
                    sent[h][j, r] = (stack, k)
                else:
                    sent[h][j, r], picked = (picked[0], None), picked[1:]
                if j == 0:
                    cols[h][0, r] = sent[h][0, r]
                if j == 1:
                    near.append((sent[h], (1, r), cols[h], (1, r), 1))
        return first

    def take_near(most):
        ready = [k for k, job in enumerate(near) if job[1] in job[0]][:most]
        taken = [near[k] for k in ready]
        near[:] = [job for k, job in enumerate(near) if k not in ready]
        jobs = []
        for source, key, store, place_in, bit in taken:
            array, view = source[key]
            jobs.append((exchange(bit), array, keep(store, place_in, view)))
        return jobs

    def slot(*jobs):
        nonlocal ended
        jobs = list(jobs) + take_near(3)
        ended = tuple(job[0](after(job[1], ended)) for job in jobs)
        for job, result in zip(jobs, ended):
            job[2](result)

    def keep(store, key, view=None):
        return lambda result: store.__setitem__(key, (result, view))

    def spread(store):
        have, bit = [0, top_bit], nodes // 4
        while bit:
            for j in sorted(have):
                if j | bit not in store:
                    near.append((store, j, store, j | bit, bit))
                have.append(j | bit)
            bit //= 2

    passing = [{} for _ in range(halves)]

    def pass_on(h, j, r):
        near.append((passing[h], (j, r), cols[h], (j, r), 1))

    def trade(h, r, js):
        def store(result):
            for k, j in enumerate(js):
                view = (result, k) if len(js) > 1 else (result, None)
                (passing if j & 1 else cols)[h][j, r] = view
                if j & 1:
                    pass_on(h, j, r)

        array = sent[h][js[0], r][0]
        return (exchange(js[0] & ~1), array, store)

    everyone = range(nodes)
    far = list(range(2, nodes))
    queue = [(r, [j, j + 1]) for r in range(pair) for j in far[::2]]
    for h in range(halves):
        spread(slab[h])
    rounds = ring - 1
    gate, loose, holding = (), (), None
    for k in range(1, rounds + 1):
        h_up, h_down = int(k > steps), int(k >= steps)
        top, bottom = ups[h_up][-1], downs[h_down][-1]
        if k <= halves:
            far_own = after(own[k - 1], [g for g in loose[-1:]])
            far_own = exchange(top_bit)(far_own)
            slab[k - 1][top_bit] = (far_own, None)
            loose = loose + (far_own,)
        if k == steps:
            first_wanted, rest = queue[:1], queue[1:]
            choose(0, first_wanted)
        if k >= steps and (k - steps) % 2 == 0 and queue:
            operator, operand, store = trade(0, *queue.pop(0))
            holding = (operator(after(operand, loose)), store)
            loose = ()
        if k == 3 or k > steps + 1:
            for operator, operand, store in take_near(4):
                result = operator(after(operand, gate, top, bottom))
                store(result)
                loose = loose + (result,)
        top, bottom = after((top, bottom), gate)
        if k > steps and (k - steps) % 2:
            gate = (holding[0],) if holding else ()
            if holding:
                holding[1](holding[0])
                holding = None
            if k == steps + 1:
                gate += (choose(0, rest + [(r, [0, 1]) for r in range(pair)]),)
        else:
            gate = ()
        ups[h_up].append(rise(top))
        downs[h_down].append(fall(bottom))
    ended = (ups[1][-1], downs[1][-1], gate, loose)
    if holding:
        holding[1](holding[0])
        ended = ended + (holding[0],)
    while queue:
        slot(trade(0, *queue.pop(0)))
    swaps = []

    def swap_job(j):
        store = passing if j & 1 else cols
        if j & 1:
            pass_on(1, j, 1)
        array, view = store[1][j, 0]
        return (swap, array, keep(store[1], (j, 1), view))

    first = choose(1, [(0, far[-1:])])
    turned_slab = None
    for j in reversed(far):
        slot(trade(1, 0, [j]), *swaps)
        if turned_slab is None:
            single = [(0, [i]) for i in far[:-1]]
            wanted = single + [(r, [0, 1]) for r in range(pair)] + [(1, far)]
            first = choose(1, wanted, first)
            whole_slab = [alone(slab[g][j]) for j in everyone for g in range(halves)]
            turned_slab = turn_blocks(after(whole_slab, first))
            ended = ended + (turned_slab[0],)
        swaps = [swap_job(j)]

    def own_rows(h):
        cases = [cols[h][j, r] for j in range(nodes) for r in range(pair)]
        piece = pick_rows(jnp.stack([z ^ node, y]), cases, pair, width)
        mine[h][0] = (piece, None)
        spread(mine[h])
        return (exchange(top_bit), piece, keep(mine[h], top_bit))

    def left_part(parts, earlier, first=False):
        blocks = [sent[h][j, r] for h, js in parts for j in js for r in range(pair)]
        theirs = [mine[h][j][0] for h, js in parts for j in js]
        return left_sum(blocks, theirs, earlier, first)

    def complete(h):
        return all((j, r) in cols[h] for j in range(nodes) for r in range(pair))

    def right_part(h):
        return right_sum(
            turned_slab, [cols[h][j, r] for j in everyone for r in range(pair)], pair
        )

    while not complete(0):
        slot()
    right_new = [right_part(0)]
    job = own_rows(0)
    ended = ended + (right_new[0],)
    slot(job, *swaps)
    lows, highs = list(everyone)[:top_bit], list(everyone)[top_bit:]
    while not complete(1) or not all(j in mine[0] for j in lows):
        slot()
    total = left_part([(0, lows)], left_old, True)
    job = own_rows(1)
    ended = ended + (total,)
    slot(job)
    right_new.append(right_part(1))
    ended = ended + (right_new[1],)
    while not all(j in mine[0] for j in everyone) or not all(j in mine[1] for j in lows):
        slot()
    total = left_part([(0, highs), (1, lows)], total)
    ended = ended + (total,)
    while near:
        slot()
    left_out = left_part([(1, highs)], total)

    right_new = jnp.stack(right_new, 1)
    right_new = jnp.where(y == 0, right_new, right_new[::-1]).reshape(right_old.shape)
    right_out = ema_decay * right_old + (1.0 - ema_decay) * right_new
    return (left_out, right_out)


def solution(mesh):
    placed = (P("dp", "node"), P("dp", None), P("node", "dp"), P("node", "dp"))
    return jax.shard_map(
        shards,
        mesh=mesh,
        in_specs=placed,
        out_specs=(P("node", "dp"), P("node", "dp")),
        check_vma=False,
    )
```
